32 devices in a mesh: depth: 2 (over x), space: 16 (over z, y, core).
Axes of the slice: x: 2, y: 2, z: 4, core: 2. Of those that a mesh axis runs over, the one named last changes fastest.
Arguments:
- c_points: float32 [2, 64, 64, 256], P('depth', None, 'space'), may hold values from -6 to 6
- adjoint_points: float32 [2, 64, 64, 256], P('depth', None, 'space'), may hold values from -6 to 6
- conv1_weight: bfloat16 [8, 64, 576], P('depth'), may hold values from -0.25 to 0.25
- conv2_weight: bfloat16 [8, 64, 576], P('depth'), may hold values from -0.25 to 0.25
- bias1: float32 [8, 64], P('depth'), may hold values from -3 to 3
Outputs:
- new_points: float32 [2, 64, 64, 256], P('depth', None, 'space')
- new_adjoints: float32 [2, 64, 64, 256], P('depth', None, 'space')
- grad_one: float32 [8, 64, 576], P('depth')
- grad_two: float32 [8, 64, 576], P('depth')
- grad_bias: float32 [8, 64], P('depth')
The draws below stay inside these ranges and needn't reach their ends.
All inputs are finite; a program needn't handle non-finite values.
Results may differ from the reference program's by a relative error of at most 0.006.
Values may be sent and summed in bfloat16 or wider, within the bound.
A program may use at most 64 MiB of HBM per device.

```python
import math
import jax
import jax.numpy as jnp
from jax import lax

CHANNELS = 64
COLS = 256
LAYERS_DEV = 4
NROWS = 64
LAYERS = 8
N_DEPTH = 2


def block_levels(stream_key, shape, split, least, top_value):
    loudness, own = 1.0, jax.random.fold_in(stream_key, 6)
    for axis_at, blocks in split:
        draws = jnp.exp(jax.random.uniform(jax.random.fold_in(own, axis_at), (blocks,), jnp.float32, least / len(split), top_value / len(split)))
        loudness = loudness * jnp.repeat(draws, shape[axis_at] // blocks).reshape([-1 if axis == axis_at else 1 for axis in range(len(shape))])
    return loudness


def scatter_about(rng, extent, width, most, split=(), kind=jnp.bfloat16):
    values = width * jax.random.normal(rng, extent, jnp.float32)
    if split:
        values = values * block_levels(rng, extent, split, -0.22, 0.18)
    return jnp.clip(values, -most, most).astype(kind)


def setup_inputs(seed: int = 0) -> dict:
    splits = jax.random.split(jax.random.key(seed), 6)
    return {
        "c_points": scatter_about(splits[0], (N_DEPTH, CHANNELS, NROWS, COLS), 1.0, 6.0, ((0, 2), (2, 16)), jnp.float32),
        "adjoint_points": scatter_about(splits[1], (N_DEPTH, CHANNELS, NROWS, COLS), 1.0, 6.0, ((0, 2), (2, 16)), jnp.float32),
        "conv1_weight": scatter_about(splits[2], (LAYERS, CHANNELS, 9 * CHANNELS), (9 * CHANNELS) ** -0.5, 0.25, ((0, 2),)),
        "conv2_weight": scatter_about(splits[3], (LAYERS, CHANNELS, 9 * CHANNELS), (9 * CHANNELS) ** -0.5, 0.25, ((0, 2),)),
        "bias1": scatter_about(splits[4], (LAYERS, CHANNELS), 0.5, 3.0, ((0, 2),), jnp.float32),
    }


STEP = 0.25

def pad_both(field):
    return jnp.pad(field, ((0, 0), (1, 1), (1, 1)))

def tap_columns(padded, height, breadth):
    pieces = [padded[:, row_off:row_off + height, col_off:col_off + breadth] for row_off in range(3) for col_off in range(3)]
    return jnp.stack(pieces, 0).reshape(-1, height * breadth)

def flip_taps(padded, height, breadth):
    pieces = [padded[:, 2 - row_off:2 - row_off + height, 2 - col_off:2 - col_off + breadth] for row_off in range(3) for col_off in range(3)]
    return jnp.stack(pieces, 0).reshape(-1, height * breadth)

def transpose_weight(weight):
    chans = weight.shape[0]
    return weight.reshape(chans, 9, chans).transpose(2, 1, 0).reshape(chans, 9 * chans)

def outer_sum(left, right):
    return lax.dot_general(left, right, (((1,), (1,)), ((), ())), preferred_element_type=jnp.float32)

def reference(c_points, adjoint_points, conv1_weight, conv2_weight, bias1):
    height = NROWS
    breadth = COLS
    chans = CHANNELS
    scale = 1.0 / math.sqrt(NROWS * COLS)
    finals = []
    starts = []
    list_one = []
    list_two = []
    list_bias = []
    for group in range(N_DEPTH):
        current = c_points[group]
        saved = []
        for depth_pos in range(LAYERS_DEV):
            layer_num = group * LAYERS_DEV + depth_pos
            padded_in = pad_both(current.astype(jnp.bfloat16))
            pre = jnp.dot(conv1_weight[layer_num], tap_columns(padded_in, height, breadth), preferred_element_type=jnp.float32) + bias1[layer_num][:, None]
            hidden = jax.nn.softplus(pre).astype(jnp.bfloat16).reshape(chans, height, breadth)
            padded_hid = pad_both(hidden)
            branch = jnp.dot(conv2_weight[layer_num], tap_columns(padded_hid, height, breadth), preferred_element_type=jnp.float32)
            current = current + STEP * branch.reshape(chans, height, breadth)
            slope = 1.0 - jnp.exp(-hidden.astype(jnp.float32).reshape(chans, -1))
            saved.append((padded_in, padded_hid, slope))
        finals.append(current)
        adjoint = adjoint_points[group]
        grads_one = []
        grads_two = []
        grads_bias = []
        for depth_pos in reversed(range(LAYERS_DEV)):
            layer_num = group * LAYERS_DEV + depth_pos
            padded_in, padded_hid, slope = saved[depth_pos]
            scaled = (STEP * adjoint).astype(jnp.bfloat16)
            hidden_adj = jnp.dot(transpose_weight(conv2_weight[layer_num]), flip_taps(pad_both(scaled), height, breadth), preferred_element_type=jnp.float32)
            pre_adj = (hidden_adj * slope).astype(jnp.bfloat16)
            back = jnp.dot(transpose_weight(conv1_weight[layer_num]), flip_taps(pad_both(pre_adj.reshape(chans, height, breadth)), height, breadth), preferred_element_type=jnp.float32)
            adjoint = adjoint + back.reshape(chans, height, breadth)
            grads_two.append(outer_sum(scaled.reshape(chans, -1), tap_columns(padded_hid, height, breadth)) * scale)
            grads_one.append(outer_sum(pre_adj, tap_columns(padded_in, height, breadth)) * scale)
            grads_bias.append(lax.optimization_barrier(jnp.sum(pre_adj.astype(jnp.float32), axis=1)) * scale)
        starts.append(adjoint)
        list_one.extend(grads_one[::-1])
        list_two.extend(grads_two[::-1])
        list_bias.extend(grads_bias[::-1])
    new_points = jnp.stack([c_points[0]] + finals[:-1], 0)
    new_adjoints = jnp.stack(starts[1:] + [adjoint_points[N_DEPTH - 1]], 0)
    return (new_points, new_adjoints, jnp.stack(list_one, 0), jnp.stack(list_two, 0), jnp.stack(list_bias, 0))
```

```python
import functools
import math

import jax
import jax.numpy as jnp
from jax import lax
from jax.experimental import pallas as pl
from jax.experimental.pallas import tpu as pltpu
from jax.sharding import PartitionSpec as P

STEP = 0.25
MESH = pl.DeviceIdType.MESH
F32 = jnp.float32
BF16 = jnp.bfloat16
ROWS = 16


def remote(src, dst, send, recv, where):
    return pltpu.make_async_remote_copy(
        src_ref=src, dst_ref=dst, send_sem=send, recv_sem=recv,
        device_id=where, device_id_type=MESH,
    )


def three_columns(value):
    breadth = value.shape[1]
    col = lax.broadcasted_iota(jnp.int32, value.shape, 1)
    before = jnp.where(col == 0, 0.0, pltpu.roll(value, 1, 1))
    after = jnp.where(col == breadth - 1, 0.0, pltpu.roll(value, breadth - 1, 1))
    return before.astype(BF16), value.astype(BF16), after.astype(BF16)


def row_products(left, right):
    return lax.dot_general(left, right, (((1,), (1,)), ((), ())), preferred_element_type=F32)


def kernel(
    dims, c_ref, q_ref, w1_ref, w2_ref, t1_ref, t2_ref, bias_ref,
    points_ref, adjoints_ref, one_ref, two_ref, gbias_ref,
    state, adj, xs, xlo, xhi, bs, blo, bhi, x3, a3, b3, e3, bst, est,
    part, landed, reduced, final, f_in, h_in,
    x_send, x_recv, b_send, b_recv, rs_send, rs_recv, ag_send, ag_recv, d_send, d_recv,
):
    tiles, groups, layers, chans, height, breadth, chunks, scale = dims
    me = lax.axis_index("space")
    depth = lax.axis_index("depth")
    first, last = me == 0, me == tiles - 1

    def cols(row, count=1):
        return slice(row * breadth, (row + count) * breadth)

    def up(buf, dst, send, recv, slot):
        return remote(
            buf.at[slot, :, cols(0, 2)], dst.at[slot], send.at[slot, 0], recv.at[slot, 0],
            {"space": jnp.maximum(me - 1, 0)},
        )

    def down(buf, dst, send, recv, slot):
        return remote(
            buf.at[slot, :, cols(height - 2, 2)], dst.at[slot], send.at[slot, 1],
            recv.at[slot, 1], {"space": jnp.minimum(me + 1, tiles - 1)},
        )

    barrier = pltpu.get_barrier_semaphore()

    def greet(dist, carry):
        pl.semaphore_signal(
            barrier, inc=1, device_id={"space": lax.rem(me + dist, tiles)}, device_id_type=MESH
        )
        return carry

    lax.fori_loop(1, tiles, greet, 0)

    @pl.when(depth > 0)
    def _():
        pl.semaphore_signal(
            barrier, inc=1, device_id={"depth": depth - 1}, device_id_type=MESH
        )

    @pl.when(depth < groups - 1)
    def _():
        pl.semaphore_signal(
            barrier, inc=1, device_id={"depth": depth + 1}, device_id_type=MESH
        )

    for row in range(height):
        own = c_ref[0, :, row, :]
        state[:, cols(row)] = own
        xs[0, :, cols(row)] = own.astype(BF16)
        own = q_ref[0, :, row, :]
        adj[:, cols(row)] = own
        bs[layers - 1, :, cols(row)] = (STEP * own).astype(BF16)
    bst[...] = jnp.zeros_like(bst)
    est[...] = jnp.zeros_like(est)

    @pl.when(first)
    def _():
        xlo[...] = jnp.zeros_like(xlo)
        blo[...] = jnp.zeros_like(blo)

    @pl.when(last)
    def _():
        xhi[...] = jnp.zeros_like(xhi)
        bhi[...] = jnp.zeros_like(bhi)

    beside = (depth > 0).astype(jnp.int32) + (depth < groups - 1).astype(jnp.int32)
    pl.semaphore_wait(barrier, tiles - 1 + beside)

    @pl.when(jnp.logical_not(first))
    def _():
        up(xs, xhi, x_send, x_recv, 0).start()
        up(bs, bhi, b_send, b_recv, layers - 1).start()

    @pl.when(jnp.logical_not(last))
    def _():
        down(xs, xlo, x_send, x_recv, 0).start()
        down(bs, blo, b_send, b_recv, layers - 1).start()

    def conv(weight, load, rows, store, done, outs):
        for row in rows:
            store(row)
            prod = jnp.dot(weight, load(row), preferred_element_type=F32)
            for tap in range(3):
                out = row - tap
                if 0 <= out < outs:
                    piece = prod[tap * chans : (tap + 1) * chans]
                    done[out] = piece if out not in done else done[out] + piece

    def forward(layer, carry):
        pre = {}

        def put(row):
            if 2 <= row < height + 2:
                value = state[:, cols(row - 2)]
            elif row < 2:
                value = xlo[layer, :, cols(row)].astype(F32)
            else:
                value = xhi[layer, :, cols(row - height - 2)].astype(F32)
            for tap, piece in enumerate(three_columns(value)):
                x3[layer, tap * chans : (tap + 1) * chans, cols(row)] = piece

        def hide(row):
            total = pre[row] + bias_ref[layer]
            value = jnp.maximum(total, 0.0) + jnp.log1p(jnp.exp(-jnp.abs(total)))
            if row == 0:
                value = jnp.where(first, 0.0, value)
            if row == height + 1:
                value = jnp.where(last, 0.0, value)
            for tap, piece in enumerate(three_columns(value)):
                a3[layer, tap * chans : (tap + 1) * chans, cols(row)] = piece

        weight = w1_ref[layer]
        load = lambda row: x3[layer, :, cols(row)]
        conv(weight, load, range(2, height + 2), put, pre, height + 2)
        for row in range(2, height):
            hide(row)

        @pl.when(jnp.logical_not(first))
        def _():
            down(xs, xlo, x_send, x_recv, layer).wait_recv()

        conv(weight, load, (1, 0), put, pre, height + 2)
        hide(0)
        hide(1)

        @pl.when(jnp.logical_not(last))
        def _():
            up(xs, xhi, x_send, x_recv, layer).wait_recv()

        conv(weight, load, (height + 2, height + 3), put, pre, height + 2)
        hide(height)
        hide(height + 1)
        branch = {}
        conv(
            w2_ref[layer], lambda row: a3[layer, :, cols(row)], range(height + 2),
            lambda row: None, branch, height,
        )
        for row in range(height):
            value = state[:, cols(row)] + STEP * branch[row]
            state[:, cols(row)] = value
            xs[layer + 1, :, cols(row)] = value.astype(BF16)
            if row == 1:

                @pl.when(jnp.logical_not(first) & (layer < layers - 1))
                def _():
                    up(xs, xhi, x_send, x_recv, layer + 1).start()

        @pl.when(jnp.logical_not(last) & (layer < layers - 1))
        def _():
            down(xs, xlo, x_send, x_recv, layer + 1).start()

        return carry

    lax.fori_loop(0, layers, forward, 0)

    send_f = remote(
        state, f_in, d_send.at[0], d_recv.at[0], {"depth": jnp.minimum(depth + 1, groups - 1)}
    )
    send_h = remote(
        adj, h_in, d_send.at[1], d_recv.at[1], {"depth": jnp.maximum(depth - 1, 0)}
    )

    @pl.when(depth < groups - 1)
    def _():
        send_f.start()

    def owner(chunk):
        return (chunk * tiles) // chunks

    mine = (me * chunks + tiles - 1) // tiles
    owning = (mine < chunks) & (owner(mine) == me)
    held = jnp.minimum(mine, chunks - 1)

    def scatter(layer, chunk):
        target = owner(chunk)
        slot = lax.rem(me - target - 1 + 2 * tiles, tiles)
        return target, lambda: remote(
            part.at[layer, chunk], landed.at[layer, slot], rs_send.at[layer, chunk],
            rs_recv.at[layer, slot], {"space": target},
        )

    def arrival(layer, slot):
        return remote(
            part.at[layer, 0], landed.at[layer, slot], rs_send.at[layer, 0],
            rs_recv.at[layer, slot], {"space": me},
        )

    def spread(layer, dist, chunk):
        return remote(
            reduced.at[layer], final.at[layer, chunk], ag_send.at[layer, dist],
            ag_recv.at[layer, chunk], {"space": lax.rem(me + dist, tiles)},
        )

    def reduce(layer):
        @pl.when(owning)
        def _():
            def add(slot, total):
                arrival(layer, slot).wait_recv()
                return total + landed[layer, slot].astype(F32)

            total = lax.fori_loop(0, tiles - 1, add, part[layer, held].astype(F32))
            total = total.astype(BF16)
            reduced[layer] = total
            final[layer, held] = total

            def send(dist, carry):
                spread(layer, dist, held).start()
                return carry

            lax.fori_loop(1, tiles, send, 0)

    def backward(step, carry):
        layer = layers - 1 - step
        hidden = {}

        def put(row):
            if 2 <= row < height + 2:
                value = STEP * adj[:, cols(row - 2)]
            elif row < 2:
                value = blo[layer, :, cols(row)].astype(F32)
            else:
                value = bhi[layer, :, cols(row - height - 2)].astype(F32)
            pieces = three_columns(value)
            for tap, piece in enumerate(pieces):
                b3[tap * chans : (tap + 1) * chans, cols(row)] = piece
                if 2 <= row < height + 2:
                    bst[tap * chans : (tap + 1) * chans, cols(row - 2 + tap)] = pieces[1]

        def slope(row):
            field = a3[layer, chans : 2 * chans, cols(row)].astype(F32)
            pieces = three_columns(hidden[row] * (1.0 - jnp.exp(-field)))
            for tap, piece in enumerate(pieces):
                e3[tap * chans : (tap + 1) * chans, cols(row)] = piece
                if 1 <= row <= height:
                    est[tap * chans : (tap + 1) * chans, cols(row - 1 + tap)] = pieces[1]

        weight = t2_ref[layer]
        load = lambda row: b3[:, cols(row)]
        conv(weight, load, range(2, height + 2), put, hidden, height + 2)
        for row in range(2, height):
            slope(row)

        @pl.when(jnp.logical_not(first))
        def _():
            down(bs, blo, b_send, b_recv, layer).wait_recv()

        conv(weight, load, (1, 0), put, hidden, height + 2)
        slope(0)
        slope(1)

        @pl.when(jnp.logical_not(last))
        def _():
            up(bs, bhi, b_send, b_recv, layer).wait_recv()

        conv(weight, load, (height + 2, height + 3), put, hidden, height + 2)
        slope(height)
        slope(height + 1)
        back = {}
        conv(
            t1_ref[layer], lambda row: e3[:, cols(row)], range(height + 2),
            lambda row: None, back, height,
        )
        after = jnp.maximum(layer - 1, 0)
        for row in range(height):
            value = adj[:, cols(row)] + back[row]
            adj[:, cols(row)] = value

            @pl.when(layer > 0)
            def _():
                bs[after, :, cols(row)] = (STEP * value).astype(BF16)

            if row == 1:

                @pl.when(jnp.logical_not(first) & (layer > 0))
                def _():
                    up(bs, bhi, b_send, b_recv, after).start()

        @pl.when(jnp.logical_not(last) & (layer > 0))
        def _():
            down(bs, blo, b_send, b_recv, after).start()

        @pl.when((layer == 0) & (depth > 0))
        def _():
            send_h.start()

        grad_two = row_products(bst[...], a3[layer])
        grad_one = row_products(est[...], x3[layer, :, breadth : (height + 3) * breadth])
        ones = jnp.ones((ROWS, (height + 2) * breadth), BF16)
        grad_bias = row_products(ones, est[0:chans])
        both = jnp.concatenate([grad_two, grad_one], axis=1).astype(BF16)
        for chunk in range(chunks - 1):
            part[layer, chunk] = both[chunk * ROWS : (chunk + 1) * ROWS]
        part[layer, chunks - 1] = jnp.zeros((ROWS, 6 * chans), BF16)
        part[layer, chunks - 1, :, 0:chans] = grad_bias.astype(BF16)

        def send(chunk, carry):
            target, copy = scatter(layer, chunk)

            @pl.when(target != me)
            def _():
                copy().start()

            return carry

        lax.fori_loop(0, chunks, send, 0)

        @pl.when(step > 0)
        def _():
            reduce(jnp.minimum(layer + 1, layers - 1))

        return carry

    lax.fori_loop(0, layers, backward, 0)
    reduce(0)

    @pl.when(depth == 0)
    def _():
        points_ref[...] = c_ref[...]

    @pl.when(depth > 0)
    def _():
        send_f.wait_recv()
        for row in range(height):
            points_ref[0, :, row, :] = f_in[:, cols(row)]

    @pl.when(depth == groups - 1)
    def _():
        adjoints_ref[...] = q_ref[...]

    @pl.when(depth < groups - 1)
    def _():
        send_h.wait_recv()
        for row in range(height):
            adjoints_ref[0, :, row, :] = h_in[:, cols(row)]

    def unpack(step, carry):
        layer = layers - 1 - step

        def landing(chunk, inner):
            @pl.when(owner(chunk) != me)
            def _():
                spread(layer, 1, chunk).wait_recv()

            return inner

        lax.fori_loop(0, chunks, landing, 0)
        per = chans // ROWS
        wide = 3 * chans
        for tap in range(3):
            for block in range(per):
                value = final[layer, tap * per + block].astype(F32) * scale
                rows = slice(block * ROWS, (block + 1) * ROWS)
                two_ref[layer, rows, tap * wide : (tap + 1) * wide] = value[:, :wide]
                one_ref[layer, rows, tap * wide : (tap + 1) * wide] = value[:, wide:]
        gbias_ref[layer] = final[layer, chunks - 1, :, 0:chans].astype(F32) * scale
        return carry

    lax.fori_loop(0, layers, unpack, 0)

    def sent(layer, carry):
        @pl.when(jnp.logical_not(first))
        def _():
            up(xs, xhi, x_send, x_recv, layer).wait_send()
            up(bs, bhi, b_send, b_recv, layer).wait_send()

        @pl.when(jnp.logical_not(last))
        def _():
            down(xs, xlo, x_send, x_recv, layer).wait_send()
            down(bs, blo, b_send, b_recv, layer).wait_send()

        def scattered(chunk, inner):
            target, copy = scatter(layer, chunk)

            @pl.when(target != me)
            def _():
                copy().wait_send()

            return inner

        lax.fori_loop(0, chunks, scattered, 0)

        @pl.when(owning)
        def _():
            def gone(dist, inner):
                spread(layer, dist, held).wait_send()
                return inner

            lax.fori_loop(1, tiles, gone, 0)

        return carry

    lax.fori_loop(0, layers, sent, 0)

    @pl.when(depth < groups - 1)
    def _():
        send_f.wait_send()

    @pl.when(depth > 0)
    def _():
        send_h.wait_send()


def stacked(weight):
    layers, chans, _ = weight.shape
    return (
        weight.reshape(layers, chans, 3, 3 * chans).transpose(0, 2, 1, 3)
        .reshape(layers, 3 * chans, 3 * chans)
    )


def stacked_back(weight):
    layers, chans, _ = weight.shape
    return (
        weight.reshape(layers, chans, 3, 3, chans)[:, :, ::-1, ::-1].transpose(0, 2, 4, 3, 1)
        .reshape(layers, 3 * chans, 3 * chans)
    )


def body(tiles, groups, c_points, adjoint_points, conv1_weight, conv2_weight, bias1):
    _, chans, height, breadth = c_points.shape
    layers = conv1_weight.shape[0]
    chunks = 3 * chans // ROWS + 1
    scale = 1.0 / math.sqrt(height * tiles * breadth)
    dims = (tiles, groups, layers, chans, height, breadth, chunks, scale)
    size = height * breadth
    wide = 3 * chans
    dma = pltpu.SemaphoreType.DMA
    vmem = pltpu.VMEM
    halo = vmem((layers, chans, 2 * breadth), BF16)
    outs = pl.pallas_call(
        functools.partial(kernel, dims),
        out_shape=(
            jax.ShapeDtypeStruct(c_points.shape, F32),
            jax.ShapeDtypeStruct(c_points.shape, F32),
            jax.ShapeDtypeStruct(conv1_weight.shape, F32),
            jax.ShapeDtypeStruct(conv1_weight.shape, F32),
            jax.ShapeDtypeStruct((layers, ROWS, chans), F32),
        ),
        in_specs=[pl.BlockSpec(memory_space=vmem)] * 7,
        out_specs=(pl.BlockSpec(memory_space=vmem),) * 5,
        scratch_shapes=[
            vmem((chans, size), F32),
            vmem((chans, size), F32),
            vmem((layers + 1, chans, size), BF16), halo, halo,
            vmem((layers, chans, size), BF16), halo, halo,
            vmem((layers, wide, size + 4 * breadth), BF16),
            vmem((layers, wide, size + 2 * breadth), BF16),
            vmem((wide, size + 4 * breadth), BF16),
            vmem((wide, size + 2 * breadth), BF16),
            vmem((wide, size + 2 * breadth), BF16),
            vmem((wide, size + 2 * breadth), BF16),
            vmem((layers, chunks, ROWS, 2 * wide), BF16),
            vmem((layers, tiles - 1, ROWS, 2 * wide), BF16),
            vmem((layers, ROWS, 2 * wide), BF16),
            vmem((layers, chunks, ROWS, 2 * wide), BF16),
            vmem((chans, size), F32),
            vmem((chans, size), F32),
            dma((layers, 2)), dma((layers, 2)), dma((layers, 2)), dma((layers, 2)),
            dma((layers, chunks)), dma((layers, tiles)),
            dma((layers, tiles)), dma((layers, chunks)),
            dma((2,)), dma((2,)),
        ],
        compiler_params=pltpu.CompilerParams(
            collective_id=0, has_side_effects=True, vmem_limit_bytes=56 * 1024 * 1024
        ),
    )(
        c_points, adjoint_points, stacked(conv1_weight), stacked(conv2_weight),
        stacked_back(conv1_weight), stacked_back(conv2_weight), bias1[:, :, None],
    )
    return outs[:4] + (outs[4][:, 0],)


def solution(mesh):
    specs = (
        P("depth", None, "space", None),
        P("depth", None, "space", None),
        P("depth", None, None),
        P("depth", None, None),
        P("depth", None),
    )
    return jax.shard_map(
        functools.partial(body, mesh.shape["space"], mesh.shape["depth"]),
        mesh=mesh, in_specs=specs, out_specs=specs, check_vma=False,
    )
```

```python
import functools
import math

import jax
import jax.numpy as jnp
from jax import lax
from jax.experimental import pallas as pl
from jax.experimental.pallas import tpu as pltpu
from jax.sharding import PartitionSpec as P

STEP = 0.25
MESH = pl.DeviceIdType.MESH
F32 = jnp.float32
BF16 = jnp.bfloat16
ROWS = 16


def remote(src, dst, send, recv, where):
    return pltpu.make_async_remote_copy(
        src_ref=src, dst_ref=dst, send_sem=send, recv_sem=recv,
        device_id=where, device_id_type=MESH,
    )


def three_columns(value):
    breadth = value.shape[1]
    col = lax.broadcasted_iota(jnp.int32, value.shape, 1)
    before = jnp.where(col == 0, 0.0, pltpu.roll(value, 1, 1))
    after = jnp.where(col == breadth - 1, 0.0, pltpu.roll(value, breadth - 1, 1))
    return before.astype(BF16), value.astype(BF16), after.astype(BF16)


def row_products(left, right):
    return lax.dot_general(left, right, (((1,), (1,)), ((), ())), preferred_element_type=F32)


def kernel(
    dims, c_ref, q_ref, raw1_ref, raw2_ref, bias_ref,
    f_in, h_in, final,
    w1_ref, w2_ref, t1_ref, t2_ref, state, adj, xs, xlo, xhi, bs, blo, bhi, x3, a3, b3, e3, bst, est,
    part, landed, reduced,
    x_send, x_recv, b_send, b_recv, rs_send, rs_recv, ag_send, ag_recv, d_send, d_recv,
):
    tiles, groups, layers, chans, height, breadth, chunks, scale = dims
    me = lax.axis_index("space")
    depth = lax.axis_index("depth")
    first, last = me == 0, me == tiles - 1

    def cols(row, count=1):
        return slice(row * breadth, (row + count) * breadth)

    def up(buf, dst, send, recv, slot):
        return remote(
            buf.at[slot, :, cols(0, 2)], dst.at[slot], send.at[slot, 0], recv.at[slot, 0],
            {"space": jnp.maximum(me - 1, 0)},
        )

    def down(buf, dst, send, recv, slot):
        return remote(
            buf.at[slot, :, cols(height - 2, 2)], dst.at[slot], send.at[slot, 1],
            recv.at[slot, 1], {"space": jnp.minimum(me + 1, tiles - 1)},
        )

    def prepare(layer):
        wide = 3 * chans
        for raw, straight, turned in ((raw1_ref, w1_ref, t1_ref), (raw2_ref, w2_ref, t2_ref)):
            full = raw[layer].astype(F32)
            weight = jnp.concatenate([full[:, t * wide : (t + 1) * wide] for t in range(3)], 0)
            straight[layer] = weight.astype(BF16)
            flat = full.T
            for tap in range(3):
                piece = jnp.concatenate(
                    [
                        flat[(3 * (2 - tap) + other) * chans : (3 * (2 - tap) + other + 1) * chans]
                        for other in (2, 1, 0)
                    ],
                    axis=1,
                )
                turned[layer, tap * chans : (tap + 1) * chans] = piece.astype(BF16)

    barrier = pltpu.get_barrier_semaphore()

    def greet(dist, carry):
        pl.semaphore_signal(
            barrier, inc=1, device_id={"space": lax.rem(me + dist, tiles)}, device_id_type=MESH
        )
        return carry

    lax.fori_loop(1, tiles, greet, 0)

    @pl.when(depth > 0)
    def _():
        pl.semaphore_signal(
            barrier, inc=1, device_id={"depth": depth - 1}, device_id_type=MESH
        )

    @pl.when(depth < groups - 1)
    def _():
        pl.semaphore_signal(
            barrier, inc=1, device_id={"depth": depth + 1}, device_id_type=MESH
        )

    for row in range(height):
        own = c_ref[0, :, row, :]
        state[:, cols(row)] = own
        xs[0, :, cols(row)] = own.astype(BF16)
        own = q_ref[0, :, row, :]
        adj[:, cols(row)] = own
        bs[layers - 1, :, cols(row)] = (STEP * own).astype(BF16)
    bst[...] = jnp.zeros_like(bst)
    est[...] = jnp.zeros_like(est)
    prepare(0)

    @pl.when(first)
    def _():
        xlo[...] = jnp.zeros_like(xlo)
        blo[...] = jnp.zeros_like(blo)

    @pl.when(last)
    def _():
        xhi[...] = jnp.zeros_like(xhi)
        bhi[...] = jnp.zeros_like(bhi)

    beside = (depth > 0).astype(jnp.int32) + (depth < groups - 1).astype(jnp.int32)
    pl.semaphore_wait(barrier, tiles - 1 + beside)

    @pl.when(jnp.logical_not(first))
    def _():
        up(xs, xhi, x_send, x_recv, 0).start()
        up(bs, bhi, b_send, b_recv, layers - 1).start()

    @pl.when(jnp.logical_not(last))
    def _():
        down(xs, xlo, x_send, x_recv, 0).start()
        down(bs, blo, b_send, b_recv, layers - 1).start()

    def conv(weight, load, rows, store, total, outs, ready):
        for row in rows:
            store(row)
            prod = jnp.dot(weight, load(row), preferred_element_type=F32)
            for tap in range(3):
                out = row - tap
                if 0 <= out < outs:
                    piece = prod[tap * chans : (tap + 1) * chans]
                    value, count = total.get(out, (None, 0))
                    total[out] = (piece if value is None else value + piece, count + 1)
                    if count == 2:
                        ready(out, total[out][0])

    low = (True, (1, 0), (1, 0))
    high = (False, (height + 2, height + 3), (height, height + 1))

    def in_pairs(run):
        def pair(step, carry):
            run(2 * step, (low, high))
            run(2 * step + 1, (high, low))
            return carry

        lax.fori_loop(0, layers // 2, pair, 0)
        if layers % 2:
            run(layers - 1, (low, high))

    def forward(layer, order):
        pre, branch, stored = {}, {}, set()

        def put(row):
            if 2 <= row < height + 2:
                value = state[:, cols(row - 2)]
            elif row < 2:
                value = xlo[layer, :, cols(row)].astype(F32)
            else:
                value = xhi[layer, :, cols(row - height - 2)].astype(F32)
            for tap, piece in enumerate(three_columns(value)):
                x3[layer, tap * chans : (tap + 1) * chans, cols(row)] = piece

        square = (chans, chans)
        diagonal = lax.broadcasted_iota(jnp.int32, square, 0) == lax.broadcasted_iota(
            jnp.int32, square, 1
        )
        row_bias = jnp.broadcast_to(bias_ref[pl.ds(layer, 1), :], square)
        bias = jnp.sum(jnp.where(diagonal, row_bias, 0.0), axis=1, keepdims=True)

        def hide(row, value):
            value = value + bias
            value = jnp.maximum(value, 0.0) + jnp.log1p(jnp.exp(-jnp.abs(value)))
            if row == 0:
                value = jnp.where(first, 0.0, value)
            if row == height + 1:
                value = jnp.where(last, 0.0, value)
            for tap, piece in enumerate(three_columns(value)):
                a3[layer, tap * chans : (tap + 1) * chans, cols(row)] = piece

        def update(row, value):
            value = state[:, cols(row)] + STEP * value
            state[:, cols(row)] = value
            xs[layer + 1, :, cols(row)] = value.astype(BF16)
            stored.add(row)
            after = jnp.minimum(layer + 1, layers - 1)
            if row in (0, 1) and {0, 1} <= stored:

                @pl.when(jnp.logical_not(first) & (layer < layers - 1))
                def _():
                    up(xs, xhi, x_send, x_recv, after).start()

            if row in (height - 2, height - 1) and {height - 2, height - 1} <= stored:

                @pl.when(jnp.logical_not(last) & (layer < layers - 1))
                def _():
                    down(xs, xlo, x_send, x_recv, after).start()

        def pre_rows(rows):
            conv(
                w1_ref[layer], lambda row: x3[layer, :, cols(row)], rows, put, pre,
                height + 2, hide,
            )

        def branch_rows(rows):
            conv(
                w2_ref[layer], lambda row: a3[layer, :, cols(row)], rows, lambda row: None,
                branch, height, update,
            )

        pre_rows(range(2, height + 2))
        branch_rows(range(2, height))

        @pl.when(layer < layers - 1)
        def _():
            prepare(jnp.minimum(layer + 1, layers - 1))

        for lower, outer, inner in order:
            if lower:

                @pl.when(jnp.logical_not(first))
                def _():
                    down(xs, xlo, x_send, x_recv, layer).wait_recv()
            else:

                @pl.when(jnp.logical_not(last))
                def _():
                    up(xs, xhi, x_send, x_recv, layer).wait_recv()

            pre_rows(outer)
            branch_rows(inner)

    in_pairs(forward)

    send_f = remote(
        state, f_in, d_send.at[0], d_recv.at[0], {"depth": jnp.minimum(depth + 1, groups - 1)}
    )
    send_h = remote(
        adj, h_in, d_send.at[1], d_recv.at[1], {"depth": jnp.maximum(depth - 1, 0)}
    )

    @pl.when(depth < groups - 1)
    def _():
        send_f.start()

    def owner(chunk):
        return (chunk * tiles) // chunks

    mine = (me * chunks + tiles - 1) // tiles
    owning = (mine < chunks) & (owner(mine) == me)
    held = jnp.minimum(mine, chunks - 1)

    def scatter(layer, chunk):
        target = owner(chunk)
        slot = lax.rem(me - target - 1 + 2 * tiles, tiles)
        return target, lambda: remote(
            part.at[layer, chunk], landed.at[layer, slot], rs_send.at[layer, chunk],
            rs_recv.at[layer, slot], {"space": target},
        )

    def arrival(layer, slot):
        return remote(
            part.at[layer, 0], landed.at[layer, slot], rs_send.at[layer, 0],
            rs_recv.at[layer, slot], {"space": me},
        )

    def spread(layer, dist, chunk):
        return remote(
            reduced.at[layer], final.at[layer, chunk], ag_send.at[layer, dist],
            ag_recv.at[layer, chunk], {"space": lax.rem(me + dist, tiles)},
        )

    def reduce(layer):
        @pl.when(owning)
        def _():
            def add(slot, total):
                arrival(layer, slot).wait_recv()
                return total + landed[layer, slot].astype(F32)

            total = lax.fori_loop(0, tiles - 1, add, part[layer, held].astype(F32))
            total = total.astype(BF16)
            reduced[layer] = total
            final[layer, held] = total

            def send(dist, carry):
                spread(layer, dist, held).start()
                return carry

            lax.fori_loop(1, tiles, send, 0)

    def pack(layer, grad, start):
        half = grad.shape[0] // 2
        both = jnp.concatenate([grad[:half], grad[half:]], axis=1).astype(BF16)
        for chunk in range(half // ROWS):
            part[layer, start + chunk] = both[chunk * ROWS : (chunk + 1) * ROWS]

    def ship(layer, start, stop):
        def send(chunk, carry):
            target, copy = scatter(layer, chunk)

            @pl.when(target != me)
            def _():
                copy().start()

            return carry

        lax.fori_loop(start, stop, send, 0)

    def backward(step, order):
        layer = layers - 1 - step
        after = jnp.maximum(layer - 1, 0)
        hidden, back, stored = {}, {}, set()

        def put(row):
            if 2 <= row < height + 2:
                value = STEP * adj[:, cols(row - 2)]
            elif row < 2:
                value = blo[layer, :, cols(row)].astype(F32)
            else:
                value = bhi[layer, :, cols(row - height - 2)].astype(F32)
            pieces = three_columns(value)
            for tap, piece in enumerate(pieces):
                b3[tap * chans : (tap + 1) * chans, cols(row)] = piece
                if 2 <= row < height + 2:
                    bst[tap * chans : (tap + 1) * chans, cols(row - 2 + tap)] = pieces[1]

        def slope(row, value):
            field = a3[layer, chans : 2 * chans, cols(row)].astype(F32)
            pieces = three_columns(value * (1.0 - jnp.exp(-field)))
            for tap, piece in enumerate(pieces):
                e3[tap * chans : (tap + 1) * chans, cols(row)] = piece
                if 1 <= row <= height:
                    est[tap * chans : (tap + 1) * chans, cols(row - 1 + tap)] = pieces[1]

        def update(row, value):
            value = adj[:, cols(row)] + value
            adj[:, cols(row)] = value
            stored.add(row)

            @pl.when(layer > 0)
            def _():
                bs[after, :, cols(row)] = (STEP * value).astype(BF16)

            if row in (0, 1) and {0, 1} <= stored:

                @pl.when(jnp.logical_not(first) & (layer > 0))
                def _():
                    up(bs, bhi, b_send, b_recv, after).start()

            if row in (height - 2, height - 1) and {height - 2, height - 1} <= stored:

                @pl.when(jnp.logical_not(last) & (layer > 0))
                def _():
                    down(bs, blo, b_send, b_recv, after).start()

        def hidden_rows(rows):
            conv(
                t2_ref[layer], lambda row: b3[:, cols(row)], rows, put, hidden,
                height + 2, slope,
            )

        def back_rows(rows):
            conv(
                t1_ref[layer], lambda row: e3[:, cols(row)], rows, lambda row: None,
                back, height, update,
            )

        hidden_rows(range(2, height + 2))
        back_rows(range(2, height))
        split = (chunks - 1) // 2
        pack(layer, row_products(bst[...], a3[layer]), 0)
        ship(layer, 0, split)
        for lower, outer, inner in order:
            if lower:

                @pl.when(jnp.logical_not(first))
                def _():
                    down(bs, blo, b_send, b_recv, layer).wait_recv()
            else:

                @pl.when(jnp.logical_not(last))
                def _():
                    up(bs, bhi, b_send, b_recv, layer).wait_recv()

            hidden_rows(outer)
            back_rows(inner)

        grad_one = row_products(est[...], x3[layer, :, breadth : (height + 3) * breadth])
        ones = jnp.ones((ROWS, (height + 2) * breadth), BF16)
        grad_bias = row_products(ones, est[0:chans])
        pack(layer, grad_one, split)
        part[layer, chunks - 1] = jnp.zeros((ROWS, 6 * chans), BF16)
        part[layer, chunks - 1, :, 0:chans] = grad_bias.astype(BF16)
        ship(layer, split, chunks)

        @pl.when((layer == 0) & (depth > 0))
        def _():
            send_h.start()

        @pl.when(step > 0)
        def _():
            reduce(jnp.minimum(layer + 1, layers - 1))

    in_pairs(backward)
    reduce(0)

    @pl.when(depth > 0)
    def _():
        send_f.wait_recv()

    @pl.when(depth < groups - 1)
    def _():
        send_h.wait_recv()

    def gathered(layer, carry):
        def landing(chunk, inner):
            @pl.when(owner(chunk) != me)
            def _():
                spread(layer, 1, chunk).wait_recv()

            return inner

        return lax.fori_loop(0, chunks, landing, carry)

    lax.fori_loop(0, layers, gathered, 0)

    def sent(layer, carry):
        @pl.when(jnp.logical_not(first))
        def _():
            up(xs, xhi, x_send, x_recv, layer).wait_send()
            up(bs, bhi, b_send, b_recv, layer).wait_send()

        @pl.when(jnp.logical_not(last))
        def _():
            down(xs, xlo, x_send, x_recv, layer).wait_send()
            down(bs, blo, b_send, b_recv, layer).wait_send()

        def scattered(chunk, inner):
            target, copy = scatter(layer, chunk)

            @pl.when(target != me)
            def _():
                copy().wait_send()

            return inner

        lax.fori_loop(0, chunks, scattered, 0)

        @pl.when(owning)
        def _():
            def gone(dist, inner):
                spread(layer, dist, held).wait_send()
                return inner

            lax.fori_loop(1, tiles, gone, 0)

        return carry

    lax.fori_loop(0, layers, sent, 0)

    @pl.when(depth < groups - 1)
    def _():
        send_f.wait_send()

    @pl.when(depth > 0)
    def _():
        send_h.wait_send()


def finish(
    dims, c_ref, q_ref, f_ref, h_ref, final,
    points_ref, adjoints_ref, one_ref, two_ref, gbias_ref,
):
    tiles, groups, layers, chans, height, breadth, chunks, scale = dims
    depth = lax.axis_index("depth")

    @pl.when(depth == 0)
    def _():
        points_ref[...] = c_ref[...]

    @pl.when(depth > 0)
    def _():
        for row in range(height):
            points_ref[0, :, row, :] = f_ref[:, row * breadth : (row + 1) * breadth]

    @pl.when(depth == groups - 1)
    def _():
        adjoints_ref[...] = q_ref[...]

    @pl.when(depth < groups - 1)
    def _():
        for row in range(height):
            adjoints_ref[0, :, row, :] = h_ref[:, row * breadth : (row + 1) * breadth]

    per = chans // ROWS
    wide = 3 * chans
    split = (chunks - 1) // 2
    for layer in range(layers):
        for out_ref, start in ((two_ref, 0), (one_ref, split)):
            for block in range(split):
                value = final[layer, start + block].astype(F32) * scale
                for at, piece in ((block, value[:, :wide]), (block + split, value[:, wide:])):
                    tap, place = at // per, at % per * ROWS
                    out_ref[layer, place : place + ROWS, tap * wide : (tap + 1) * wide] = piece
        value = final[layer, chunks - 1].astype(F32) * scale
        gbias_ref[layer : layer + 1, :] = value[0:1, 0:chans]


def body(tiles, groups, c_points, adjoint_points, conv1_weight, conv2_weight, bias1):
    _, chans, height, breadth = c_points.shape
    layers = conv1_weight.shape[0]
    chunks = 3 * chans // ROWS + 1
    scale = 1.0 / math.sqrt(height * tiles * breadth)
    dims = (tiles, groups, layers, chans, height, breadth, chunks, scale)
    size = height * breadth
    wide = 3 * chans
    dma = pltpu.SemaphoreType.DMA
    vmem = pltpu.VMEM
    halo = vmem((layers, chans, 2 * breadth), BF16)
    outs = pl.pallas_call(
        functools.partial(kernel, dims),
        out_shape=(
            jax.ShapeDtypeStruct((chans, size), F32),
            jax.ShapeDtypeStruct((chans, size), F32),
            jax.ShapeDtypeStruct((layers, chunks, ROWS, 2 * wide), BF16),
        ),
        in_specs=[pl.BlockSpec(memory_space=vmem)] * 5,
        out_specs=(pl.BlockSpec(memory_space=vmem),) * 3,
        scratch_shapes=[
            vmem((layers, wide, wide), BF16), vmem((layers, wide, wide), BF16),
            vmem((layers, wide, wide), BF16), vmem((layers, wide, wide), BF16),
            vmem((chans, size), F32),
            vmem((chans, size), F32),
            vmem((layers + 1, chans, size), BF16), halo, halo,
            vmem((layers, chans, size), BF16), halo, halo,
            vmem((layers, wide, size + 4 * breadth), BF16),
            vmem((layers, wide, size + 2 * breadth), BF16),
            vmem((wide, size + 4 * breadth), BF16),
            vmem((wide, size + 2 * breadth), BF16),
            vmem((wide, size + 2 * breadth), BF16),
            vmem((wide, size + 2 * breadth), BF16),
            vmem((layers, chunks, ROWS, 2 * wide), BF16),
            vmem((layers, tiles - 1, ROWS, 2 * wide), BF16),
            vmem((layers, ROWS, 2 * wide), BF16),
            dma((layers, 2)), dma((layers, 2)), dma((layers, 2)), dma((layers, 2)),
            dma((layers, chunks)), dma((layers, tiles)),
            dma((layers, tiles)), dma((layers, chunks)),
            dma((2,)), dma((2,)),
        ],
        compiler_params=pltpu.CompilerParams(
            collective_id=0, has_side_effects=True, vmem_limit_bytes=56 * 1024 * 1024
        ),
    )(c_points, adjoint_points, conv1_weight, conv2_weight, bias1)
    return pl.pallas_call(
        functools.partial(finish, dims),
        out_shape=(
            jax.ShapeDtypeStruct(c_points.shape, F32),
            jax.ShapeDtypeStruct(c_points.shape, F32),
            jax.ShapeDtypeStruct(conv1_weight.shape, F32),
            jax.ShapeDtypeStruct(conv1_weight.shape, F32),
            jax.ShapeDtypeStruct(bias1.shape, F32),
        ),
        in_specs=[pl.BlockSpec(memory_space=vmem)] * 5,
        out_specs=(pl.BlockSpec(memory_space=vmem),) * 5,
        compiler_params=pltpu.CompilerParams(vmem_limit_bytes=32 * 1024 * 1024),
    )(c_points, adjoint_points, *outs)


def solution(mesh):
    specs = (
        P("depth", None, "space", None),
        P("depth", None, "space", None),
        P("depth", None, None),
        P("depth", None, None),
        P("depth", None),
    )
    return jax.shard_map(
        functools.partial(body, mesh.shape["space"], mesh.shape["depth"]),
        mesh=mesh, in_specs=specs, out_specs=specs, check_vma=False,
    )
```

```python
import functools
import math

import jax
import jax.numpy as jnp
from jax import lax
from jax.experimental import pallas as pl
from jax.experimental.pallas import tpu as pltpu
from jax.sharding import PartitionSpec as P

STEP = 0.25
MESH = pl.DeviceIdType.MESH
F32 = jnp.float32
BF16 = jnp.bfloat16
ROWS = 16


def remote(src, dst, send, recv, where):
    return pltpu.make_async_remote_copy(
        src_ref=src, dst_ref=dst, send_sem=send, recv_sem=recv,
        device_id=where, device_id_type=MESH,
    )


def sharing(tiles, chunks):
    levels = 4
    plane = tiles // levels
    per = -(-chunks // plane)
    assert levels * plane == tiles and plane > 1 and per <= levels
    return levels, plane, per


def three_columns(value):
    breadth = value.shape[1]
    col = lax.broadcasted_iota(jnp.int32, value.shape, 1)
    before = jnp.where(col == 0, 0.0, pltpu.roll(value, 1, 1))
    after = jnp.where(col == breadth - 1, 0.0, pltpu.roll(value, breadth - 1, 1))
    return before.astype(BF16), value.astype(BF16), after.astype(BF16)


def row_products(left, right):
    return lax.dot_general(left, right, (((1,), (1,)), ((), ())), preferred_element_type=F32)


def kernel(
    dims, c_ref, q_ref, raw1_ref, raw2_ref, bias_ref,
    f_in, h_in, final,
    w1_ref, w2_ref, t1_ref, t2_ref, state, adj, xs, xlo, xhi, bs, blo, bhi, x3, a3, b3, e3, bst, est,
    part, land_plane, middle, land_line, reduced,
    x_send, x_recv, b_send, b_recv, p_send, p_recv, l_send, l_recv, r_send, r_recv,
    g_send, g_recv, d_send, d_recv,
):
    tiles, groups, layers, chans, height, breadth, chunks, scale = dims
    me = lax.axis_index("space")
    depth = lax.axis_index("depth")
    first, last = me == 0, me == tiles - 1

    def cols(row, count=1):
        return slice(row * breadth, (row + count) * breadth)

    def up(buf, dst, send, recv, slot):
        return remote(
            buf.at[slot, :, cols(0, 2)], dst.at[slot], send.at[slot, 0], recv.at[slot, 0],
            {"space": jnp.maximum(me - 1, 0)},
        )

    def down(buf, dst, send, recv, slot):
        return remote(
            buf.at[slot, :, cols(height - 2, 2)], dst.at[slot], send.at[slot, 1],
            recv.at[slot, 1], {"space": jnp.minimum(me + 1, tiles - 1)},
        )

    def prepare(layer):
        wide = 3 * chans
        for raw, straight, turned in ((raw1_ref, w1_ref, t1_ref), (raw2_ref, w2_ref, t2_ref)):
            full = raw[layer].astype(F32)
            weight = jnp.concatenate([full[:, t * wide : (t + 1) * wide] for t in range(3)], 0)
            straight[layer] = weight.astype(BF16)
            flat = full.T
            for tap in range(3):
                piece = jnp.concatenate(
                    [
                        flat[(3 * (2 - tap) + other) * chans : (3 * (2 - tap) + other + 1) * chans]
                        for other in (2, 1, 0)
                    ],
                    axis=1,
                )
                turned[layer, tap * chans : (tap + 1) * chans] = piece.astype(BF16)

    barrier = pltpu.get_barrier_semaphore()

    def greet(dist, carry):
        pl.semaphore_signal(
            barrier, inc=1, device_id={"space": lax.rem(me + dist, tiles)}, device_id_type=MESH
        )
        return carry

    lax.fori_loop(1, tiles, greet, 0)

    @pl.when(depth > 0)
    def _():
        pl.semaphore_signal(
            barrier, inc=1, device_id={"depth": depth - 1}, device_id_type=MESH
        )

    @pl.when(depth < groups - 1)
    def _():
        pl.semaphore_signal(
            barrier, inc=1, device_id={"depth": depth + 1}, device_id_type=MESH
        )

    for row in range(height):
        own = c_ref[0, :, row, :]
        state[:, cols(row)] = own
        xs[0, :, cols(row)] = own.astype(BF16)
        own = q_ref[0, :, row, :]
        adj[:, cols(row)] = own
        bs[layers - 1, :, cols(row)] = (STEP * own).astype(BF16)
    bst[...] = jnp.zeros_like(bst)
    est[...] = jnp.zeros_like(est)
    prepare(0)

    @pl.when(first)
    def _():
        xlo[...] = jnp.zeros_like(xlo)
        blo[...] = jnp.zeros_like(blo)

    @pl.when(last)
    def _():
        xhi[...] = jnp.zeros_like(xhi)
        bhi[...] = jnp.zeros_like(bhi)

    beside = (depth > 0).astype(jnp.int32) + (depth < groups - 1).astype(jnp.int32)
    pl.semaphore_wait(barrier, tiles - 1 + beside)

    @pl.when(jnp.logical_not(first))
    def _():
        up(xs, xhi, x_send, x_recv, 0).start()
        up(bs, bhi, b_send, b_recv, layers - 1).start()

    @pl.when(jnp.logical_not(last))
    def _():
        down(xs, xlo, x_send, x_recv, 0).start()
        down(bs, blo, b_send, b_recv, layers - 1).start()

    def conv(weight, load, rows, store, total, outs, ready):
        for row in rows:
            store(row)
            prod = jnp.dot(weight, load(row), preferred_element_type=F32)
            for tap in range(3):
                out = row - tap
                if 0 <= out < outs:
                    piece = prod[tap * chans : (tap + 1) * chans]
                    value, count = total.get(out, (None, 0))
                    total[out] = (piece if value is None else value + piece, count + 1)
                    if count == 2:
                        ready(out, total[out][0])

    low = (True, (1, 0), (1, 0))
    high = (False, (height + 2, height + 3), (height, height + 1))

    def in_pairs(run):
        def pair(step, carry):
            run(2 * step, (low, high))
            run(2 * step + 1, (high, low))
            return carry

        lax.fori_loop(0, layers // 2, pair, 0)
        if layers % 2:
            run(layers - 1, (low, high))

    def forward(layer, order):
        pre, branch, stored = {}, {}, set()

        def put(row):
            if 2 <= row < height + 2:
                value = state[:, cols(row - 2)]
            elif row < 2:
                value = xlo[layer, :, cols(row)].astype(F32)
            else:
                value = xhi[layer, :, cols(row - height - 2)].astype(F32)
            for tap, piece in enumerate(three_columns(value)):
                x3[layer, tap * chans : (tap + 1) * chans, cols(row)] = piece

        square = (chans, chans)
        diagonal = lax.broadcasted_iota(jnp.int32, square, 0) == lax.broadcasted_iota(
            jnp.int32, square, 1
        )
        row_bias = jnp.broadcast_to(bias_ref[pl.ds(layer, 1), :], square)
        bias = jnp.sum(jnp.where(diagonal, row_bias, 0.0), axis=1, keepdims=True)

        def hide(row, value):
            value = value + bias
            value = jnp.maximum(value, 0.0) + jnp.log1p(jnp.exp(-jnp.abs(value)))
            if row == 0:
                value = jnp.where(first, 0.0, value)
            if row == height + 1:
                value = jnp.where(last, 0.0, value)
            for tap, piece in enumerate(three_columns(value)):
                a3[layer, tap * chans : (tap + 1) * chans, cols(row)] = piece

        def update(row, value):
            value = state[:, cols(row)] + STEP * value
            state[:, cols(row)] = value
            xs[layer + 1, :, cols(row)] = value.astype(BF16)
            stored.add(row)
            after = jnp.minimum(layer + 1, layers - 1)
            if row in (0, 1) and {0, 1} <= stored:

                @pl.when(jnp.logical_not(first) & (layer < layers - 1))
                def _():
                    up(xs, xhi, x_send, x_recv, after).start()

            if row in (height - 2, height - 1) and {height - 2, height - 1} <= stored:

                @pl.when(jnp.logical_not(last) & (layer < layers - 1))
                def _():
                    down(xs, xlo, x_send, x_recv, after).start()

        def pre_rows(rows):
            conv(
                w1_ref[layer], lambda row: x3[layer, :, cols(row)], rows, put, pre,
                height + 2, hide,
            )

        def branch_rows(rows):
            conv(
                w2_ref[layer], lambda row: a3[layer, :, cols(row)], rows, lambda row: None,
                branch, height, update,
            )

        pre_rows(range(2, height + 2))
        branch_rows(range(2, height))

        @pl.when(layer < layers - 1)
        def _():
            prepare(jnp.minimum(layer + 1, layers - 1))

        for lower, outer, inner in order:
            if lower:

                @pl.when(jnp.logical_not(first))
                def _():
                    down(xs, xlo, x_send, x_recv, layer).wait_recv()
            else:

                @pl.when(jnp.logical_not(last))
                def _():
                    up(xs, xhi, x_send, x_recv, layer).wait_recv()

            pre_rows(outer)
            branch_rows(inner)

    in_pairs(forward)

    send_f = remote(
        state, f_in, d_send.at[0], d_recv.at[0], {"depth": jnp.minimum(depth + 1, groups - 1)}
    )
    send_h = remote(
        adj, h_in, d_send.at[1], d_recv.at[1], {"depth": jnp.maximum(depth - 1, 0)}
    )

    @pl.when(depth < groups - 1)
    def _():
        send_f.start()

    levels, plane, per = sharing(tiles, chunks)
    level, place = lax.div(me, plane), lax.rem(me, plane)
    held = jnp.clip(chunks - place * per, 0, per)

    def chunk_of(idx):
        return jnp.minimum(place * per + idx, chunks - 1)

    def plane_copy(layer, chunk):
        target, idx = lax.div(chunk, per), lax.rem(chunk, per)
        slot = lax.rem(place - target - 1 + 2 * plane, plane) * per + idx
        return target, lambda: remote(
            part.at[layer, chunk], land_plane.at[layer, slot], p_send.at[layer, chunk],
            p_recv.at[layer, slot], {"space": level * plane + target},
        )

    def line_copy(layer, idx, slot):
        return remote(
            middle.at[layer, idx], land_line.at[layer, slot], l_send.at[layer, idx],
            l_recv.at[layer, slot], {"space": idx * plane + place},
        )

    def line_back(layer, dist, idx):
        return remote(
            reduced.at[layer], final.at[layer, chunk_of(idx)], r_send.at[layer, dist],
            r_recv.at[layer, idx], {"space": lax.rem(level + dist, levels) * plane + place},
        )

    def plane_back(layer, idx, dist, chunk):
        return remote(
            final.at[layer, chunk], final.at[layer, chunk], g_send.at[layer, idx * plane + dist],
            g_recv.at[layer, chunk], {"space": level * plane + lax.rem(place + dist, plane)},
        )

    def sum_plane(layer):
        for idx in range(per):

            @pl.when(idx < held)
            def _():
                total = part[layer, chunk_of(idx)].astype(F32)
                for source in range(plane - 1):
                    slot = source * per + idx
                    remote(
                        part.at[layer, 0], land_plane.at[layer, slot], p_send.at[layer, 0],
                        p_recv.at[layer, slot], {"space": me},
                    ).wait_recv()
                    total = total + land_plane[layer, slot].astype(F32)
                middle[layer, idx] = total.astype(BF16)

                @pl.when(level != idx)
                def _():
                    line_copy(layer, idx, lax.rem(level - idx - 1 + 2 * levels, levels)).start()

    def sum_line(layer):
        @pl.when(level < held)
        def _():
            own = jnp.minimum(level, per - 1)
            total = middle[layer, own].astype(F32)
            for slot in range(levels - 1):
                line_copy(layer, 0, slot).wait_recv()
                total = total + land_line[layer, slot].astype(F32)
            total = total.astype(BF16)
            reduced[layer] = total
            final[layer, chunk_of(own)] = total
            for dist in range(1, levels):
                line_back(layer, dist, own).start()

    def spread(layer):
        for idx in range(per):

            @pl.when(idx < held)
            def _():
                @pl.when(level != idx)
                def _():
                    line_back(layer, 1, idx).wait_recv()

                for dist in range(1, plane):
                    plane_back(layer, idx, dist, chunk_of(idx)).start()

    def pack(layer, grad, start):
        half = grad.shape[0] // 2
        both = jnp.concatenate([grad[:half], grad[half:]], axis=1).astype(BF16)
        for chunk in range(half // ROWS):
            part[layer, start + chunk] = both[chunk * ROWS : (chunk + 1) * ROWS]

    def ship(layer, start, stop):
        def send(chunk, carry):
            target, copy = plane_copy(layer, chunk)

            @pl.when(target != place)
            def _():
                copy().start()

            return carry

        lax.fori_loop(start, stop, send, 0)

    def backward(step, order):
        layer = layers - 1 - step
        after = jnp.maximum(layer - 1, 0)
        hidden, back, stored = {}, {}, set()

        def put(row):
            if 2 <= row < height + 2:
                value = STEP * adj[:, cols(row - 2)]
            elif row < 2:
                value = blo[layer, :, cols(row)].astype(F32)
            else:
                value = bhi[layer, :, cols(row - height - 2)].astype(F32)
            pieces = three_columns(value)
            for tap, piece in enumerate(pieces):
                b3[tap * chans : (tap + 1) * chans, cols(row)] = piece
                if 2 <= row < height + 2:
                    bst[tap * chans : (tap + 1) * chans, cols(row - 2 + tap)] = pieces[1]

        def slope(row, value):
            field = a3[layer, chans : 2 * chans, cols(row)].astype(F32)
            pieces = three_columns(value * (1.0 - jnp.exp(-field)))
            for tap, piece in enumerate(pieces):
                e3[tap * chans : (tap + 1) * chans, cols(row)] = piece
                if 1 <= row <= height:
                    est[tap * chans : (tap + 1) * chans, cols(row - 1 + tap)] = pieces[1]

        def update(row, value):
            value = adj[:, cols(row)] + value
            adj[:, cols(row)] = value
            stored.add(row)

            @pl.when(layer > 0)
            def _():
                bs[after, :, cols(row)] = (STEP * value).astype(BF16)

            if row in (0, 1) and {0, 1} <= stored:

                @pl.when(jnp.logical_not(first) & (layer > 0))
                def _():
                    up(bs, bhi, b_send, b_recv, after).start()

            if row in (height - 2, height - 1) and {height - 2, height - 1} <= stored:

                @pl.when(jnp.logical_not(last) & (layer > 0))
                def _():
                    down(bs, blo, b_send, b_recv, after).start()

        def hidden_rows(rows):
            conv(
                t2_ref[layer], lambda row: b3[:, cols(row)], rows, put, hidden,
                height + 2, slope,
            )

        def back_rows(rows):
            conv(
                t1_ref[layer], lambda row: e3[:, cols(row)], rows, lambda row: None,
                back, height, update,
            )

        hidden_rows(range(2, height + 2))
        back_rows(range(2, height))
        split = (chunks - 1) // 2
        pack(layer, row_products(bst[...], a3[layer]), 0)
        ship(layer, 0, split)

        @pl.when(step > 1)
        def _():
            sum_line(jnp.minimum(layer + 2, layers - 1))

        for lower, outer, inner in order:
            if lower:

                @pl.when(jnp.logical_not(first))
                def _():
                    down(bs, blo, b_send, b_recv, layer).wait_recv()
            else:

                @pl.when(jnp.logical_not(last))
                def _():
                    up(bs, bhi, b_send, b_recv, layer).wait_recv()

            hidden_rows(outer)
            back_rows(inner)

        grad_one = row_products(est[...], x3[layer, :, breadth : (height + 3) * breadth])
        ones = jnp.ones((ROWS, (height + 2) * breadth), BF16)
        grad_bias = row_products(ones, est[0:chans])
        pack(layer, grad_one, split)
        part[layer, chunks - 1] = jnp.zeros((ROWS, 6 * chans), BF16)
        part[layer, chunks - 1, :, 0:chans] = grad_bias.astype(BF16)
        ship(layer, split, chunks)

        @pl.when((layer == 0) & (depth > 0))
        def _():
            send_h.start()

        @pl.when(step > 0)
        def _():
            sum_plane(jnp.minimum(layer + 1, layers - 1))

        @pl.when(step > 1)
        def _():
            spread(jnp.minimum(layer + 2, layers - 1))

    in_pairs(backward)
    if layers > 1:
        sum_line(1)
    sum_plane(0)
    if layers > 1:
        spread(1)
    sum_line(0)
    spread(0)

    @pl.when(depth > 0)
    def _():
        send_f.wait_recv()

    @pl.when(depth < groups - 1)
    def _():
        send_h.wait_recv()

    def gathered(layer, carry):
        def landing(chunk, inner):
            @pl.when(lax.div(chunk, per) != place)
            def _():
                plane_back(layer, 0, 1, chunk).wait_recv()

            return inner

        return lax.fori_loop(0, chunks, landing, carry)

    lax.fori_loop(0, layers, gathered, 0)

    def sent(layer, carry):
        @pl.when(jnp.logical_not(first))
        def _():
            up(xs, xhi, x_send, x_recv, layer).wait_send()
            up(bs, bhi, b_send, b_recv, layer).wait_send()

        @pl.when(jnp.logical_not(last))
        def _():
            down(xs, xlo, x_send, x_recv, layer).wait_send()
            down(bs, blo, b_send, b_recv, layer).wait_send()

        def scattered(chunk, inner):
            target, copy = plane_copy(layer, chunk)

            @pl.when(target != place)
            def _():
                copy().wait_send()

            return inner

        lax.fori_loop(0, chunks, scattered, 0)
        for idx in range(per):

            @pl.when(idx < held)
            def _():
                @pl.when(level != idx)
                def _():
                    line_copy(layer, idx, 0).wait_send()

                for dist in range(1, plane):
                    plane_back(layer, idx, dist, chunk_of(idx)).wait_send()

        @pl.when(level < held)
        def _():
            for dist in range(1, levels):
                line_back(layer, dist, jnp.minimum(level, per - 1)).wait_send()

        return carry

    lax.fori_loop(0, layers, sent, 0)

    @pl.when(depth < groups - 1)
    def _():
        send_f.wait_send()

    @pl.when(depth > 0)
    def _():
        send_h.wait_send()


def finish(
    dims, c_ref, q_ref, f_hbm, h_hbm, final_hbm,
    points_ref, adjoints_ref, one_ref, two_ref, gbias_ref,
    f_ref, h_ref, final, sems,
):
    tiles, groups, layers, chans, height, breadth, chunks, scale = dims
    loads = [
        pltpu.make_async_copy(src, dst, sems.at[at])
        for at, (src, dst) in enumerate(((f_hbm, f_ref), (h_hbm, h_ref), (final_hbm, final)))
    ]
    for load in loads:
        load.start()
    for load in loads:
        load.wait()
    depth = lax.axis_index("depth")

    @pl.when(depth == 0)
    def _():
        points_ref[...] = c_ref[...]

    @pl.when(depth > 0)
    def _():
        for row in range(height):
            points_ref[0, :, row, :] = f_ref[:, row * breadth : (row + 1) * breadth]

    @pl.when(depth == groups - 1)
    def _():
        adjoints_ref[...] = q_ref[...]

    @pl.when(depth < groups - 1)
    def _():
        for row in range(height):
            adjoints_ref[0, :, row, :] = h_ref[:, row * breadth : (row + 1) * breadth]

    per = chans // ROWS
    wide = 3 * chans
    split = (chunks - 1) // 2
    for layer in range(layers):
        for out_ref, start in ((two_ref, 0), (one_ref, split)):
            for block in range(split):
                value = final[layer, start + block].astype(F32) * scale
                for at, piece in ((block, value[:, :wide]), (block + split, value[:, wide:])):
                    tap, place = at // per, at % per * ROWS
                    out_ref[layer, place : place + ROWS, tap * wide : (tap + 1) * wide] = piece
        value = final[layer, chunks - 1].astype(F32) * scale
        gbias_ref[layer : layer + 1, :] = value[0:1, 0:chans]


def body(tiles, groups, c_points, adjoint_points, conv1_weight, conv2_weight, bias1):
    _, chans, height, breadth = c_points.shape
    layers = conv1_weight.shape[0]
    chunks = 3 * chans // ROWS + 1
    scale = 1.0 / math.sqrt(height * tiles * breadth)
    dims = (tiles, groups, layers, chans, height, breadth, chunks, scale)
    size = height * breadth
    wide = 3 * chans
    levels, plane, per = sharing(tiles, chunks)
    dma = pltpu.SemaphoreType.DMA
    vmem = pltpu.VMEM
    halo = vmem((layers, chans, 2 * breadth), BF16)
    outs = pl.pallas_call(
        functools.partial(kernel, dims),
        out_shape=(
            jax.ShapeDtypeStruct((chans, size), F32),
            jax.ShapeDtypeStruct((chans, size), F32),
            jax.ShapeDtypeStruct((layers, chunks, ROWS, 2 * wide), BF16),
        ),
        in_specs=[pl.BlockSpec(memory_space=vmem)] * 5,
        out_specs=(pl.BlockSpec(memory_space=vmem),) * 3,
        scratch_shapes=[
            vmem((layers, wide, wide), BF16), vmem((layers, wide, wide), BF16),
            vmem((layers, wide, wide), BF16), vmem((layers, wide, wide), BF16),
            vmem((chans, size), F32),
            vmem((chans, size), F32),
            vmem((layers + 1, chans, size), BF16), halo, halo,
            vmem((layers, chans, size), BF16), halo, halo,
            vmem((layers, wide, size + 4 * breadth), BF16),
            vmem((layers, wide, size + 2 * breadth), BF16),
            vmem((wide, size + 4 * breadth), BF16),
            vmem((wide, size + 2 * breadth), BF16),
            vmem((wide, size + 2 * breadth), BF16),
            vmem((wide, size + 2 * breadth), BF16),
            vmem((layers, chunks, ROWS, 2 * wide), BF16),
            vmem((layers, (plane - 1) * per, ROWS, 2 * wide), BF16),
            vmem((layers, per, ROWS, 2 * wide), BF16),
            vmem((layers, levels - 1, ROWS, 2 * wide), BF16),
            vmem((layers, ROWS, 2 * wide), BF16),
            dma((layers, 2)), dma((layers, 2)), dma((layers, 2)), dma((layers, 2)),
            dma((layers, chunks)), dma((layers, (plane - 1) * per)),
            dma((layers, per)), dma((layers, levels - 1)),
            dma((layers, levels)), dma((layers, per)),
            dma((layers, per * plane)), dma((layers, chunks)),
            dma((2,)), dma((2,)),
        ],
        compiler_params=pltpu.CompilerParams(
            collective_id=0, has_side_effects=True, vmem_limit_bytes=56 * 1024 * 1024
        ),
    )(c_points, adjoint_points, conv1_weight, conv2_weight, bias1)
    return pl.pallas_call(
        functools.partial(finish, dims),
        out_shape=(
            jax.ShapeDtypeStruct(c_points.shape, F32),
            jax.ShapeDtypeStruct(c_points.shape, F32),
            jax.ShapeDtypeStruct(conv1_weight.shape, F32),
            jax.ShapeDtypeStruct(conv1_weight.shape, F32),
            jax.ShapeDtypeStruct(bias1.shape, F32),
        ),
        in_specs=[pl.BlockSpec(memory_space=vmem)] * 2 + [pl.BlockSpec(memory_space=pl.ANY)] * 3,
        out_specs=(pl.BlockSpec(memory_space=vmem),) * 5,
        scratch_shapes=[
            vmem((chans, size), F32), vmem((chans, size), F32),
            vmem((layers, chunks, ROWS, 2 * wide), BF16), dma((3,)),
        ],
        compiler_params=pltpu.CompilerParams(vmem_limit_bytes=60 * 1024 * 1024),
    )(c_points, adjoint_points, *outs)


def solution(mesh):
    specs = (
        P("depth", None, "space", None),
        P("depth", None, "space", None),
        P("depth", None, None),
        P("depth", None, None),
        P("depth", None),
    )
    return jax.shard_map(
        functools.partial(body, mesh.shape["space"], mesh.shape["depth"]),
        mesh=mesh, in_specs=specs, out_specs=specs, check_vma=False,
    )
```
